32 devices in a mesh: day: 4 (over y, x), lon: 8 (over z, core).
Axes of the slice: x: 2, y: 2, z: 4, core: 2. Of those that a mesh axis runs over, the one named last changes fastest.
Arguments:
- observed: bfloat16 [512, 32, 1024], P('day', None, 'lon'), may hold values from -6 to 6
- decay_rate: float32 [32, 1024], P(None, 'lon'), may hold values from 0.000546875 to 0.077
- drain_factor: float32 [512, 32], P('day'), may hold values from 0.5 to 1
- smoothing: float32 [32, 1024], P(None, 'lon'), may hold values from 0.12 to 0.245
- land_mask: int32 [32, 1024], P(None, 'lon'), may hold values 0 or 1
- zone_ids: int32 [32, 8], P(('day', 'lon')), may hold values from 0 to 7
- kernels: bfloat16 [8, 512, 512], replicated, may hold values from -0.25 to 0.25
Outputs:
- zone_series: bfloat16 [512, 32, 1024], P(None, ('day', 'lon'))
The draws below stay inside these ranges and needn't reach their ends.
All inputs are finite; a program needn't handle non-finite values. No bound on the sum of `land_mask` on one device may be relied on, other than what follows from the above.
Results may differ from the reference program's by a relative error of at most 0.0049.
Values may be sent and summed in bfloat16 or wider, within the bound.
A program may use at most 192 MiB of HBM per device.

```python
import math
import jax
import jax.numpy as jnp
from jax import lax

PASSES = 4
ZONES = 8
DAYS = 512
LAT = 32
LON = 1024
TILES = 8


def draw_decay_rate(key, part):
    key = jax.random.fold_in(key, 11)
    key_slow, key_fast, key_pick = jax.random.split(key, 3)
    log_ten = math.log(10.0)
    slow_rate = jnp.exp(jax.random.uniform(key_slow, (LAT, LON), jnp.float32, math.log(log_ten / (8.0 * DAYS)), math.log(log_ten / DAYS)))
    fast_rate = jnp.exp(jax.random.uniform(key_fast, (LAT, LON), jnp.float32, math.log(log_ten / 50.0), math.log(log_ten / 30.0)))
    fast_share = 0.5
    chosen_fast = jax.random.bernoulli(key_pick, fast_share, (LAT, LON))
    return jnp.where(chosen_fast, fast_rate, slow_rate).astype(jnp.float32)


def draw_drain_factor(key, part):
    key = jax.random.fold_in(key, 23)
    key_days, key_depth = jax.random.split(key)
    event_days = jax.random.randint(key_days, (3, LAT), 0, DAYS)
    event_hit = jnp.any(jnp.arange(DAYS)[:, None, None] == event_days[None], axis=1)
    drop_depth = jax.random.uniform(key_depth, (DAYS, LAT), jnp.float32, 0.5, 0.8)
    return jnp.where(event_hit, drop_depth, 1.0).astype(jnp.float32)


def set_ends(entries, rng, smallest, top_value):
    spot = [jax.random.randint(jax.random.fold_in(rng, axis), (), 0, length) for axis, length in enumerate(entries.shape)]
    widest = entries.shape.index(max(entries.shape))
    neighbour = spot[:widest] + [(spot[widest] + 1) % entries.shape[widest]] + spot[widest + 1:]
    return entries.at[tuple(spot)].set(smallest).at[tuple(neighbour)].set(top_value)


def shard_levels(key, shape, cuts, smallest, largest):
    gain = 1.0
    for dim, shards_of in cuts:
        steps = jax.random.uniform(jax.random.fold_in(jax.random.fold_in(key, 6), dim), (shards_of,), jnp.float32, smallest / len(cuts), largest / len(cuts))
        gain = gain * jnp.repeat(jnp.exp(steps), shape[dim] // shards_of).reshape((-1,) + (1,) * (len(shape) - 1 - dim))
    return gain


def bell_draw(rng, shape, scale, limit, pieces=(), kind=jnp.bfloat16):
    loudness = shard_levels(rng, shape, pieces, -0.22, 0.18) if pieces else 1.0
    entries = jax.random.normal(rng, shape, jnp.float32) * scale * loudness
    return jnp.minimum(jnp.maximum(entries, -limit), limit).astype(kind)


def setup_inputs(seed: int = 0) -> dict:
    seeds = jax.random.split(jax.random.key(seed), 8)
    return {
        "observed": bell_draw(seeds[0], (DAYS, LAT, LON), 1.0, 6.0, ((0, 4), (2, 8))),
        "decay_rate": draw_decay_rate(jax.random.fold_in(seeds[7], 71), 0),
        "drain_factor": draw_drain_factor(jax.random.fold_in(seeds[7], 71), 0),
        "smoothing": jnp.clip(0.12 + 0.125 * jax.random.uniform(seeds[3], (LAT, LON), jnp.float32) ** shard_levels(seeds[3], (LAT, LON), ((1, 8),), -0.2, 0.2), 0.12, 0.245),
        "land_mask": set_ends((jax.random.randint(seeds[4], (LAT, LON), 0, 4) < 3).astype(jnp.int32), jax.random.fold_in(seeds[4], 1), 0, 1),
        "zone_ids": set_ends(jax.random.randint(seeds[5], (LAT, TILES), 0, ZONES), jax.random.fold_in(seeds[5], 1), 0, ZONES - 1).astype(jnp.int32),
        "kernels": bell_draw(seeds[6], (ZONES, DAYS, DAYS), DAYS ** -0.5, 0.25),
    }


def lat_pair(values):
    northern = jnp.concatenate([values[..., :1, :], values[..., :-1, :]], axis=-2)
    southern = jnp.concatenate([values[..., 1:, :], values[..., -1:, :]], axis=-2)
    return (northern, southern)

def smooth(surface, smoothing, land_float):
    for repeat in range(PASSES):
        eastern = jnp.roll(surface, -1, axis=-1)
        western = jnp.roll(surface, 1, axis=-1)
        northern, southern = lat_pair(surface)
        surface = land_float * (surface + smoothing * (eastern + western + northern + southern - 4.0 * surface))
    return surface

def reference(observed, decay_rate, drain_factor, smoothing, land_mask, zone_ids, kernels):
    persist = jnp.exp(-decay_rate)
    inject = jnp.sqrt(1.0 - persist * persist)
    land_float = land_mask.astype(jnp.float32)

    def advance(moisture, inputs):
        day_obs, day_drain = inputs
        moisture = persist * day_drain[:, None] * moisture + inject * day_obs.astype(jnp.float32)
        return (moisture, smooth(land_float * moisture, smoothing, land_float).astype(jnp.bfloat16))
    start = jnp.zeros(decay_rate.shape, jnp.float32)
    final_state, series = lax.scan(advance, start, (observed, drain_factor))
    row_major = jnp.moveaxis(series, 1, 0)

    def project_row(inputs):
        row_series, row_zones = inputs
        blocks = row_series.reshape(DAYS, TILES, 128).astype(jnp.float32)
        chosen = kernels[row_zones].astype(jnp.float32)
        result = jnp.einsum('kts,skc->tkc', chosen, blocks, precision=lax.Precision.HIGHEST)
        return result.reshape(DAYS, LON).astype(jnp.bfloat16)
    projected = lax.map(project_row, (row_major, zone_ids))
    return jnp.moveaxis(projected, 0, 1)
```

```python
import functools

import jax
import jax.numpy as jnp
from jax import lax
from jax.experimental import pallas as pl
from jax.experimental.pallas import tpu as pltpu
from jax.sharding import PartitionSpec as P

MESH = pl.DeviceIdType.MESH
F32 = jnp.float32
RING = 4


def remote(src, dst, send, recv, device):
    return pltpu.make_async_remote_copy(
        src_ref=src, dst_ref=dst, send_sem=send, recv_sem=recv,
        device_id=device, device_id_type=MESH,
    )


def series_kernel(
    nd, nl,
    obs, decay, drain, smoothing, land, gathered,
    drain_t, drain_cum, nat, local, summary, summary_in, summary_t, strip_in,
    params_t, halo_out, halo_in, gain_self, gain_side, fade, carry_t, rings, blocks,
    sum_send, sum_recv, strip_send, strip_recv, par_send, par_recv,
    halo_send, halo_recv, row_send, row_recv, own_sem,
):
    days, rows, cells = obs.shape
    count = nd * nl
    me_d, me_l = lax.axis_index("day"), lax.axis_index("lon")
    me = me_d * nl + me_l
    east, west = lax.rem(me_l + 1, nl), lax.rem(me_l + nl - 1, nl)
    barrier = pltpu.get_barrier_semaphore()

    @pl.loop(1, count)
    def _(k):
        other = lax.rem(me + k, count)
        pl.semaphore_signal(
            barrier, inc=1, device_id=(other // nl, lax.rem(other, nl)), device_id_type=MESH
        )

    def turned(plane):
        if rows < 128:
            plane = jnp.concatenate([plane, jnp.zeros((128 - rows, cells), F32)], axis=0)
        return plane.T

    land_f = land[...].astype(F32)
    params_t[0, 8:136, :] = turned(decay[...])
    params_t[1, 8:136, :] = turned(land_f * (1.0 - 4.0 * smoothing[...]))
    params_t[2, 8:136, :] = turned(land_f * smoothing[...])
    drain_t[...] = drain[...].T
    lane = lax.broadcasted_iota(jnp.int32, (rows, days), 1)
    cum = drain_t[...]
    step = 1
    while step < days:
        cum = cum * jnp.where(lane >= step, pltpu.roll(cum, step, 1), 1.0)
        step *= 2
    drain_cum[...] = cum

    part = min(rows, 32)

    @pl.loop(0, rows // part)
    def _(b):
        band = pl.ds(pl.multiple_of(b * part, part), part)
        persist = jnp.exp(-decay[band, :])
        inject = jnp.sqrt(1.0 - persist * persist) * land[band, :].astype(F32)

        def chunk(c, level):
            factors = pltpu.roll(drain_t[band, :], lax.rem(days - 8 * c, days), 1)
            for k in range(8):
                keep = persist * factors[:, k : k + 1]
                level = keep * level + inject * obs[8 * c + k, band, :].astype(F32)
                start = pl.multiple_of((8 * c + k) * rows + b * part, part)
                nat[pl.ds(start, part), :] = level
            return level

        level = lax.fori_loop(0, days // 8, chunk, jnp.zeros((part, cells), F32))
        summary[1, band, :] = level
        summary[0, band, :] = jnp.exp(-float(days) * decay[band, :]) * drain_cum[band, days - 1 : days]

    summary_t[0] = turned(summary[0])
    summary_t[1] = turned(summary[1])

    pl.semaphore_wait(barrier, count - 1)

    copies = []
    for k in range(1, nd):
        there = lax.rem(me_d + k, nd)
        copies.append(remote(summary, summary_in.at[k], sum_send.at[k], sum_recv.at[k], (there, me_l)))
        copies.append(remote(summary_t.at[:, 120:128, :], strip_in.at[0, k], strip_send.at[0, k], strip_recv.at[0, k], (there, east)))
        copies.append(remote(summary_t.at[:, 0:8, :], strip_in.at[1, k], strip_send.at[1, k], strip_recv.at[1, k], (there, west)))
    copies.append(remote(params_t.at[:, 128:136, :], params_t.at[:, 0:8, :], par_send.at[0], par_recv.at[0], (me_d, east)))
    copies.append(remote(params_t.at[:, 8:16, :], params_t.at[:, 136:144, :], par_send.at[1], par_recv.at[1], (me_d, west)))
    for copy in copies:
        copy.start()

    @pl.loop(0, rows // 2)
    def _(i):
        first = nat[pl.ds(2 * i, days, stride=rows), :].T
        second = nat[pl.ds(2 * i + 1, days, stride=rows), :].T
        local[2 * i] = first
        local[2 * i + 1] = second
        halo_out[0, i] = jnp.concatenate([first[124:128], second[124:128]], axis=0)
        halo_out[1, i] = jnp.concatenate([first[0:4], second[0:4]], axis=0)

    copies.append(remote(halo_out.at[0], halo_in.at[0], halo_send.at[0], halo_recv.at[0], (me_d, east)))
    copies.append(remote(halo_out.at[1], halo_in.at[1], halo_send.at[1], halo_recv.at[1], (me_d, west)))
    copies[-2].start()
    copies[-1].start()

    def column(table, r):
        return pltpu.roll(table, lax.rem(128 - r, 128), 1)[:, 0:1]

    def spread(table, r):
        return jnp.broadcast_to(column(table, r), (table.shape[0], 128))

    ages = -(lax.broadcasted_iota(jnp.int32, (1, 128), 1) + 1).astype(F32)

    def faded(table, r):
        return jnp.exp(spread(table, r) * ages) * drain_cum[pl.ds(r, 1), :]

    @pl.loop(0, rows)
    def _(r):
        gain_self[r, 8:136, :] = spread(params_t[1, 8:136, :], r)
        gain_side[r, 8:136, :] = spread(params_t[2, 8:136, :], r)
        fade[r] = faded(params_t[0, 8:136, :], r)

    rings[...] = jnp.zeros_like(rings)

    for copy in copies:
        copy.wait()

    carry = jnp.zeros((rows, cells), F32)
    carry_w = jnp.zeros((8, 128), F32)
    carry_e = jnp.zeros((8, 128), F32)
    for k in range(nd - 1, 0, -1):
        used = k <= me_d
        carry = jnp.where(used, summary_in[k, 0] * carry + summary_in[k, 1], carry)
        carry_w = jnp.where(used, strip_in[0, k, 0] * carry_w + strip_in[0, k, 1], carry_w)
        carry_e = jnp.where(used, strip_in[1, k, 0] * carry_e + strip_in[1, k, 1], carry_e)
    carry_t[0:8, :] = carry_w
    carry_t[8:136, :] = turned(carry)
    carry_t[136:144, :] = carry_e

    def smooth(p, j):
        above, here, below = (
            lax.rem(jnp.maximum(j - 1, 0), RING),
            lax.rem(j, RING),
            lax.rem(jnp.minimum(j + 1, rows - 1), RING),
        )
        around = (
            rings[p - 1, here, 9:153, :] + rings[p - 1, here, 7:151, :]
            + rings[p - 1, above, 8:152, :] + rings[p - 1, below, 8:152, :]
        )
        return gain_self[j] * rings[p - 1, here, 8:152, :] + gain_side[j] * around

    @pl.loop(0, rows + 4)
    def _(i):
        @pl.when(i < rows)
        def _():
            slot = lax.rem(i, RING)
            odd = lax.rem(i, 2) == 1
            enter = spread(carry_t[...], i)
            rings[0, slot, 16:144, :] = local[i] + fade[i] * enter[8:136]
            low, high = halo_in[0, i // 2], halo_in[1, i // 2]
            low = jnp.where(odd, low, pltpu.roll(low, 4, 0))
            high = jnp.where(odd, pltpu.roll(high, 4, 0), high)
            rings[0, slot, 8:16, :] = low + faded(params_t[0, 0:8, :], i) * enter[0:8]
            rings[0, slot, 144:152, :] = high + faded(params_t[0, 136:144, :], i) * enter[136:144]
            gain_self[i, 0:8, :] = spread(params_t[1, 0:8, :], i)
            gain_self[i, 136:144, :] = spread(params_t[1, 136:144, :], i)
            gain_side[i, 0:8, :] = spread(params_t[2, 0:8, :], i)
            gain_side[i, 136:144, :] = spread(params_t[2, 136:144, :], i)

        for p in range(1, 5):
            j = i - p

            @pl.when(jnp.logical_and(j >= 0, j < rows))
            def _():
                new = smooth(p, j)
                if p < 4:
                    rings[p, lax.rem(j, RING), 8:152, :] = new
                else:
                    blocks[j] = new[8:136].astype(jnp.bfloat16)

    spot = gathered.at[me_l, :, pl.ds(pl.multiple_of(me_d * days, days), days)]

    def row_copy(k):
        other = lax.rem(me + k, count)
        return remote(
            blocks.at[other], spot, row_send.at[k], row_recv.at[k],
            (other // nl, lax.rem(other, nl)),
        )

    @pl.loop(1, count)
    def _(k):
        row_copy(k).start()

    mine = pltpu.make_async_copy(blocks.at[me], spot, own_sem)
    mine.start()
    mine.wait()

    @pl.loop(1, count)
    def _(k):
        row_copy(k).wait()


def zone_kernel(zone_ids, kernel, block, out):
    out[...] = lax.dot_general(
        kernel[0], block[0], (((1,), (1,)), ((), ())), preferred_element_type=F32
    ).astype(out.dtype)


def body(nd, nl, observed, decay_rate, drain_factor, smoothing, land_mask, zone_ids, kernels):
    days, rows, cells = observed.shape
    count = nd * nl
    total = kernels.shape[1]
    assert days == 128 and cells == 128 and rows == count
    vmem = pl.BlockSpec(memory_space=pltpu.VMEM)
    dma = pltpu.SemaphoreType.DMA
    gathered = pl.pallas_call(
        functools.partial(series_kernel, nd, nl),
        out_shape=jax.ShapeDtypeStruct((nl, cells, total), jnp.bfloat16),
        in_specs=[vmem] * 5,
        out_specs=pl.BlockSpec(memory_space=pl.ANY),
        scratch_shapes=[
            pltpu.VMEM((rows, days), F32),
            pltpu.VMEM((rows, days), F32),
            pltpu.VMEM((days * rows, cells), F32),
            pltpu.VMEM((rows, cells, days), F32),
            pltpu.VMEM((2, rows, cells), F32),
            pltpu.VMEM((nd, 2, rows, cells), F32),
            pltpu.VMEM((2, cells, 128), F32),
            pltpu.VMEM((2, nd, 2, 8, 128), F32),
            pltpu.VMEM((3, 144, 128), F32),
            pltpu.VMEM((2, rows // 2, 8, days), F32),
            pltpu.VMEM((2, rows // 2, 8, days), F32),
            pltpu.VMEM((rows, 144, 128), F32),
            pltpu.VMEM((rows, 144, 128), F32),
            pltpu.VMEM((rows, 128, 128), F32),
            pltpu.VMEM((144, 128), F32),
            pltpu.VMEM((4, RING, 160, 128), F32),
            pltpu.VMEM((rows, cells, days), jnp.bfloat16),
            dma((nd,)), dma((nd,)),
            dma((2, nd)), dma((2, nd)),
            dma((2,)), dma((2,)),
            dma((2,)), dma((2,)),
            dma((count,)), dma((count,)),
            dma,
        ],
        compiler_params=pltpu.CompilerParams(
            collective_id=0, has_side_effects=True, vmem_limit_bytes=60 * 2**20
        ),
        name="series",
    )(observed, decay_rate, drain_factor, smoothing, land_mask)
    out = pl.pallas_call(
        zone_kernel,
        out_shape=jax.ShapeDtypeStruct((total, nl * cells), jnp.bfloat16),
        grid_spec=pltpu.PrefetchScalarGridSpec(
            num_scalar_prefetch=1,
            grid=(nl,),
            in_specs=[
                pl.BlockSpec((1, total, total), lambda k, zones: (zones[0, k], 0, 0)),
                pl.BlockSpec((1, cells, total), lambda k, zones: (k, 0, 0)),
            ],
            out_specs=pl.BlockSpec((total, cells), lambda k, zones: (0, k)),
        ),
        compiler_params=pltpu.CompilerParams(vmem_limit_bytes=32 * 2**20),
        name="zones",
    )(zone_ids, kernels, gathered)
    return out.reshape(total, 1, nl * cells)


def solution(mesh):
    placed = (
        P("day", None, "lon"),
        P(None, "lon"),
        P("day", None),
        P(None, "lon"),
        P(None, "lon"),
        P(("day", "lon"), None),
        P(),
    )
    return jax.shard_map(
        functools.partial(body, mesh.shape["day"], mesh.shape["lon"]),
        mesh=mesh, in_specs=placed, out_specs=P(None, ("day", "lon"), None), check_vma=False,
    )
```

```python
import functools

import jax
import jax.numpy as jnp
from jax import lax
from jax.experimental import pallas as pl
from jax.experimental.pallas import tpu as pltpu
from jax.sharding import PartitionSpec as P

MESH = pl.DeviceIdType.MESH
F32 = jnp.float32
RING = 4


def remote(src, dst, send, recv, device):
    return pltpu.make_async_remote_copy(
        src_ref=src, dst_ref=dst, send_sem=send, recv_sem=recv,
        device_id=device, device_id_type=MESH,
    )


def series_kernel(
    nd, nl,
    zones, obs, decay, drain, smoothing, land, kernels, out,
    drain_cum, nat, local, summary, summary_in, summary_t, strip_in,
    params_t, halo_out, halo_in, gain_self, gain_side, carry_t, rings, blocks,
    kernels_in, gathered, result,
    sum_send, sum_recv, strip_send, strip_recv, par_send, par_recv,
    halo_send, halo_recv, row_send, row_recv, own_sem, kernels_sem, out_sem,
):
    days, rows, cells = obs.shape
    count = nd * nl
    me_d, me_l = lax.axis_index("day"), lax.axis_index("lon")
    me = me_d * nl + me_l
    east, west = lax.rem(me_l + 1, nl), lax.rem(me_l + nl - 1, nl)
    fetch = pltpu.make_async_copy(kernels, kernels_in, kernels_sem)
    fetch.start()
    kept = gain_self.shape[0]
    barrier = pltpu.get_barrier_semaphore()

    @pl.loop(1, count)
    def _(k):
        other = lax.rem(me + k, count)
        pl.semaphore_signal(
            barrier, inc=1, device_id=(other // nl, lax.rem(other, nl)), device_id_type=MESH
        )

    def turned(plane):
        if rows < 128:
            plane = jnp.concatenate([plane, jnp.zeros((128 - rows, cells), F32)], axis=0)
        return plane.T

    land_f = land[...].astype(F32)
    params_t[0, 8:136, :] = turned(decay[...])
    params_t[1, 8:136, :] = turned(land_f * (1.0 - 4.0 * smoothing[...]))
    params_t[2, 8:136, :] = turned(land_f * smoothing[...])
    lane = lax.broadcasted_iota(jnp.int32, (rows, days), 1)
    cum = drain[...]
    step = 1
    while step < days:
        cum = cum * jnp.where(lane >= step, pltpu.roll(cum, step, 1), 1.0)
        step *= 2
    drain_cum[...] = cum

    part = min(rows, 32)

    @pl.loop(0, rows // part)
    def _(b):
        band = pl.ds(pl.multiple_of(b * part, part), part)
        persist = jnp.exp(-decay[band, :])
        inject = jnp.sqrt(1.0 - persist * persist) * land[band, :].astype(F32)

        def chunk(c, level):
            factors = pltpu.roll(drain[band, :], lax.rem(days - 8 * c, days), 1)
            for k in range(8):
                keep = persist * factors[:, k : k + 1]
                level = keep * level + inject * obs[8 * c + k, band, :].astype(F32)
                start = pl.multiple_of((8 * c + k) * rows + b * part, part)
                nat[pl.ds(start, part), :] = level
            return level

        level = lax.fori_loop(0, days // 8, chunk, jnp.zeros((part, cells), F32))
        summary[1, band, :] = level
        summary[0, band, :] = jnp.exp(-float(days) * decay[band, :]) * drain_cum[band, days - 1 : days]

    summary_t[0] = turned(summary[0])
    summary_t[1] = turned(summary[1])

    pl.semaphore_wait(barrier, count - 1)

    copies = []
    for k in range(1, nd):
        there = lax.rem(me_d + k, nd)
        copies.append(remote(summary, summary_in.at[k], sum_send.at[k], sum_recv.at[k], (there, me_l)))
        copies.append(remote(summary_t.at[:, 120:128, :], strip_in.at[0, k], strip_send.at[0, k], strip_recv.at[0, k], (there, east)))
        copies.append(remote(summary_t.at[:, 0:8, :], strip_in.at[1, k], strip_send.at[1, k], strip_recv.at[1, k], (there, west)))
    copies.append(remote(params_t.at[:, 128:136, :], params_t.at[:, 0:8, :], par_send.at[0], par_recv.at[0], (me_d, east)))
    copies.append(remote(params_t.at[:, 8:16, :], params_t.at[:, 136:144, :], par_send.at[1], par_recv.at[1], (me_d, west)))
    for copy in copies:
        copy.start()

    @pl.loop(0, rows // 2)
    def _(i):
        first = nat[pl.ds(2 * i, days, stride=rows), :].T
        second = nat[pl.ds(2 * i + 1, days, stride=rows), :].T
        local[2 * i] = first
        local[2 * i + 1] = second
        halo_out[0, i] = jnp.concatenate([first[124:128], second[124:128]], axis=0)
        halo_out[1, i] = jnp.concatenate([first[0:4], second[0:4]], axis=0)

    copies.append(remote(halo_out.at[0], halo_in.at[0], halo_send.at[0], halo_recv.at[0], (me_d, east)))
    copies.append(remote(halo_out.at[1], halo_in.at[1], halo_send.at[1], halo_recv.at[1], (me_d, west)))
    copies[-2].start()
    copies[-1].start()

    def column(table, r):
        return pltpu.roll(table, lax.rem(128 - r, 128), 1)[:, 0:1]

    def spread(table, r):
        return jnp.broadcast_to(column(table, r), (table.shape[0], 128))

    ages = -(lax.broadcasted_iota(jnp.int32, (1, 128), 1) + 1).astype(F32)

    def faded(table, r):
        return jnp.exp(spread(table, r) * ages) * drain_cum[pl.ds(r, 1), :]

    @pl.loop(0, rows // 8)
    def _(b):
        turn = lax.rem(128 - 8 * b, 128)
        for which in range(3):
            table = pltpu.roll(params_t[which, 8:136, :], turn, 1)
            for k in range(8):
                r = 8 * b + k
                wide = jnp.broadcast_to(table[:, k : k + 1], (128, 128))
                if which == 0:
                    nat[pl.ds(pl.multiple_of(r * 128, 128), 128), :] = (
                        jnp.exp(wide * ages) * drain_cum[pl.ds(r, 1), :]
                    )
                elif kept == rows:
                    (gain_self if which == 1 else gain_side)[r, 8:136, :] = wide

    rings[...] = jnp.zeros_like(rings)

    for copy in copies:
        copy.wait()

    carry = jnp.zeros((rows, cells), F32)
    carry_w = jnp.zeros((8, 128), F32)
    carry_e = jnp.zeros((8, 128), F32)
    for k in range(nd - 1, 0, -1):
        used = k <= me_d
        carry = jnp.where(used, summary_in[k, 0] * carry + summary_in[k, 1], carry)
        carry_w = jnp.where(used, strip_in[0, k, 0] * carry_w + strip_in[0, k, 1], carry_w)
        carry_e = jnp.where(used, strip_in[1, k, 0] * carry_e + strip_in[1, k, 1], carry_e)
    carry_t[0:8, :] = carry_w
    carry_t[8:136, :] = turned(carry)
    carry_t[136:144, :] = carry_e

    spot = gathered.at[me_l, :, pl.ds(pl.multiple_of(me_d * days, days), days)]
    mine = pltpu.make_async_copy(blocks.at[me], spot, own_sem)

    def row_copy(k):
        other = lax.rem(me + k, count)
        return remote(
            blocks.at[other], spot, row_send.at[k], row_recv.at[k],
            (other // nl, lax.rem(other, nl)),
        )

    back = me_l < nl // 2

    def row(i):
        return jnp.where(back, rows - 1 - i, i)

    first = jnp.where(back, rows - nl * (me_d + 1), nl * me_d)

    def smooth(p, i, low, high):
        above, here, below = (
            lax.rem(jnp.maximum(i - 1, low), RING),
            lax.rem(i, RING),
            lax.rem(jnp.minimum(i + 1, high - 1), RING),
        )
        gain = lax.rem(row(i), kept)
        around = (
            rings[p - 1, here, 9:153, :] + rings[p - 1, here, 7:151, :]
            + rings[p - 1, above, 8:152, :] + rings[p - 1, below, 8:152, :]
        )
        return gain_self[gain] * rings[p - 1, here, 8:152, :] + gain_side[gain] * around

    def enter_row(i):
        r = row(i)
        slot, gain = lax.rem(i, RING), lax.rem(r, kept)
        odd = lax.rem(r, 2) == 1
        enter = spread(carry_t[...], r)
        fade = nat[pl.ds(pl.multiple_of(r * 128, 128), 128), :]
        rings[0, slot, 16:144, :] = local[r] + fade * enter[8:136]
        low, high = halo_in[0, r // 2], halo_in[1, r // 2]
        low = jnp.where(odd, low, pltpu.roll(low, 4, 0))
        high = jnp.where(odd, pltpu.roll(high, 4, 0), high)
        rings[0, slot, 8:16, :] = low + faded(params_t[0, 0:8, :], r) * enter[0:8]
        rings[0, slot, 144:152, :] = high + faded(params_t[0, 136:144, :], r) * enter[136:144]
        if kept == rows:
            parts = (slice(0, 8), slice(136, 144))
        else:
            parts = (slice(0, 144),)
        for part in parts:
            gain_self[gain, part, :] = spread(params_t[1, part, :], r)
            gain_side[gain, part, :] = spread(params_t[2, part, :], r)

    @pl.loop(0, 2)
    def _(segment):
        begin = segment == 0
        low = jnp.where(begin, jnp.maximum(first - 4, 0), 0)
        high = jnp.where(begin, rows, jnp.where(first == 0, 0, jnp.minimum(first + 4, rows)))
        from_row = jnp.where(begin, first, 0)
        to_row = jnp.where(begin, rows, first)

        @pl.loop(low, jnp.where(high > low, high + 4, low))
        def _(i):
            @pl.when(i < high)
            def _():
                enter_row(i)

            for p in range(1, 5):
                j = i - p

                if p < 4:
                    @pl.when(jnp.logical_and(j >= low, j < high))
                    def _():
                        rings[p, lax.rem(j, RING), 8:152, :] = smooth(p, j, low, high)
                else:
                    @pl.when(jnp.logical_and(j >= from_row, j < to_row))
                    def _():
                        r = row(j)
                        blocks[r] = smooth(p, j, low, high)[8:136].astype(jnp.bfloat16)

                        @pl.when(r == me)
                        def _():
                            mine.start()

                        @pl.when(r != me)
                        def _():
                            row_copy(lax.rem(r - me + count, count)).start()

    fetch.wait()
    mine.wait()

    def result_copy(tile):
        part = pl.ds(pl.multiple_of(tile * cells, cells), cells)
        return pltpu.make_async_copy(result.at[:, part], out.at[:, part], out_sem.at[tile])

    @pl.loop(0, nl)
    def _(m):
        tile = lax.rem(me_l + m, nl)
        for d in range(nd):
            k = lax.rem(me - d * nl - tile + count, count)

            @pl.when(k > 0)
            def _():
                row_copy(k).wait_recv()

        zone = zones[0, tile]
        result[:, pl.ds(pl.multiple_of(tile * cells, cells), cells)] = lax.dot_general(
            kernels_in[zone], gathered[tile], (((1,), (1,)), ((), ())),
            preferred_element_type=F32,
        ).astype(result.dtype)
        result_copy(tile).start()

    @pl.loop(1, count)
    def _(k):
        row_copy(k).wait_send()

    @pl.loop(0, nl)
    def _(tile):
        result_copy(tile).wait()


def body(nd, nl, observed, decay_rate, drain_factor, smoothing, land_mask, zone_ids, kernels):
    days, rows, cells = observed.shape
    count = nd * nl
    total = kernels.shape[1]
    assert days == 128 and cells == 128 and rows == count
    vmem = pl.BlockSpec(memory_space=pltpu.VMEM)
    dma = pltpu.SemaphoreType.DMA
    kept = rows if rows <= 32 else 8
    out = pl.pallas_call(
        functools.partial(series_kernel, nd, nl),
        out_shape=jax.ShapeDtypeStruct((total, nl * cells), jnp.bfloat16),
        in_specs=[pl.BlockSpec(memory_space=pltpu.SMEM)] + [vmem] * 5
        + [pl.BlockSpec(memory_space=pl.ANY)],
        out_specs=pl.BlockSpec(memory_space=pl.ANY),
        scratch_shapes=[
            pltpu.VMEM((rows, days), F32),
            pltpu.VMEM((days * rows, cells), F32),
            pltpu.VMEM((rows, cells, days), F32),
            pltpu.VMEM((2, rows, cells), F32),
            pltpu.VMEM((nd, 2, rows, cells), F32),
            pltpu.VMEM((2, cells, 128), F32),
            pltpu.VMEM((2, nd, 2, 8, 128), F32),
            pltpu.VMEM((3, 144, 128), F32),
            pltpu.VMEM((2, rows // 2, 8, days), F32),
            pltpu.VMEM((2, rows // 2, 8, days), F32),
            pltpu.VMEM((kept, 144, 128), F32),
            pltpu.VMEM((kept, 144, 128), F32),
            pltpu.VMEM((144, 128), F32),
            pltpu.VMEM((4, RING, 160, 128), F32),
            pltpu.VMEM((rows, cells, days), jnp.bfloat16),
            pltpu.VMEM(kernels.shape, jnp.bfloat16),
            pltpu.VMEM((nl, cells, total), jnp.bfloat16),
            pltpu.VMEM((total, nl * cells), jnp.bfloat16),
            dma((nd,)), dma((nd,)),
            dma((2, nd)), dma((2, nd)),
            dma((2,)), dma((2,)),
            dma((2,)), dma((2,)),
            dma((count,)), dma((count,)),
            dma, dma, dma((nl,)),
        ],
        compiler_params=pltpu.CompilerParams(
            collective_id=0, has_side_effects=True, vmem_limit_bytes=62 * 2**20
        ),
        name="series",
    )(zone_ids, observed, decay_rate, drain_factor.T, smoothing, land_mask, kernels)
    return out.reshape(total, 1, nl * cells)


def solution(mesh):
    placed = (
        P("day", None, "lon"),
        P(None, "lon"),
        P("day", None),
        P(None, "lon"),
        P(None, "lon"),
        P(("day", "lon"), None),
        P(),
    )
    return jax.shard_map(
        functools.partial(body, mesh.shape["day"], mesh.shape["lon"]),
        mesh=mesh, in_specs=placed, out_specs=P(None, ("day", "lon"), None), check_vma=False,
    )
```

```python
import functools

import jax
import jax.numpy as jnp
from jax import lax
from jax.experimental import pallas as pl
from jax.experimental.pallas import tpu as pltpu
from jax.sharding import PartitionSpec as P

MESH = pl.DeviceIdType.MESH
F32 = jnp.float32
RING = 4
WIDE = 24 * 8


def remote(src, dst, send, recv, device):
    return pltpu.make_async_remote_copy(
        src_ref=src, dst_ref=dst, send_sem=send, recv_sem=recv,
        device_id=device, device_id_type=MESH,
    )


def series_kernel(
    nd, nl,
    zones, obs, decay, drain, smoothing, land, kernels, out,
    drain_cum, nat, local, summary, summary_in, summary_t, strip_in,
    params_t, halo_out, halo_in, weave, plain, gain_self, gain_side, carry_t, rings, blocks,
    kernels_in, gathered, result,
    sum_send, sum_recv, strip_send, strip_recv, par_send, par_recv,
    halo_send, halo_recv, row_send, row_recv, own_sem, kernels_sem, out_sem,
):
    days, rows, cells = obs.shape
    count = nd * nl
    me_d, me_l = lax.axis_index("day"), lax.axis_index("lon")
    me = me_d * nl + me_l
    east, west = lax.rem(me_l + 1, nl), lax.rem(me_l + nl - 1, nl)
    fetch = pltpu.make_async_copy(kernels, kernels_in, kernels_sem)
    fetch.start()
    kept = gain_self.shape[0]
    barrier = pltpu.get_barrier_semaphore()

    @pl.loop(1, count)
    def _(k):
        other = lax.rem(me + k, count)
        pl.semaphore_signal(
            barrier, inc=1, device_id=(other // nl, lax.rem(other, nl)), device_id_type=MESH
        )

    def turned(plane):
        if rows < 128:
            plane = jnp.concatenate([plane, jnp.zeros((128 - rows, cells), F32)], axis=0)
        return plane.T

    land_f = land[...].astype(F32)
    params_t[0, 8:136, :] = turned(decay[...])
    params_t[1, 8:136, :] = turned(land_f * (1.0 - 4.0 * smoothing[...]))
    params_t[2, 8:136, :] = turned(land_f * smoothing[...])
    lane = lax.broadcasted_iota(jnp.int32, (rows, days), 1)
    cum = drain[...]
    step = 1
    while step < days:
        cum = cum * jnp.where(lane >= step, pltpu.roll(cum, step, 1), 1.0)
        step *= 2
    drain_cum[...] = cum

    part = min(rows, 32)

    @pl.loop(0, rows // part)
    def _(b):
        band = pl.ds(pl.multiple_of(b * part, part), part)
        persist = jnp.exp(-decay[band, :])
        inject = jnp.sqrt(1.0 - persist * persist) * land[band, :].astype(F32)

        def chunk(c, level):
            factors = pltpu.roll(drain[band, :], lax.rem(days - 8 * c, days), 1)
            for k in range(8):
                keep = persist * factors[:, k : k + 1]
                level = keep * level + inject * obs[8 * c + k, band, :].astype(F32)
                start = pl.multiple_of((8 * c + k) * rows + b * part, part)
                nat[pl.ds(start, part), :] = level
            return level

        level = lax.fori_loop(0, days // 8, chunk, jnp.zeros((part, cells), F32))
        summary[1, band, :] = level
        summary[0, band, :] = jnp.exp(-float(days) * decay[band, :]) * drain_cum[band, days - 1 : days]

    summary_t[0] = turned(summary[0])
    summary_t[1] = turned(summary[1])

    pl.semaphore_wait(barrier, count - 1)

    copies = []
    for k in range(1, nd):
        there = lax.rem(me_d + k, nd)
        copies.append(remote(summary, summary_in.at[k], sum_send.at[k], sum_recv.at[k], (there, me_l)))
        copies.append(remote(summary_t.at[:, 120:128, :], strip_in.at[0, k], strip_send.at[0, k], strip_recv.at[0, k], (there, east)))
        copies.append(remote(summary_t.at[:, 0:8, :], strip_in.at[1, k], strip_send.at[1, k], strip_recv.at[1, k], (there, west)))
    params_copies = [
        remote(params_t.at[:, 128:136, :], params_t.at[:, 0:8, :], par_send.at[0], par_recv.at[0], (me_d, east)),
        remote(params_t.at[:, 8:16, :], params_t.at[:, 136:144, :], par_send.at[1], par_recv.at[1], (me_d, west)),
    ]
    for copy in params_copies + copies:
        copy.start()

    @pl.loop(0, rows // 2)
    def _(i):
        first = nat[pl.ds(2 * i, days, stride=rows), :].T
        second = nat[pl.ds(2 * i + 1, days, stride=rows), :].T
        local[2 * i, 8:136, :] = first
        local[2 * i + 1, 8:136, :] = second
        halo_out[0, i] = jnp.concatenate([first[124:128], second[124:128]], axis=0)
        halo_out[1, i] = jnp.concatenate([first[0:4], second[0:4]], axis=0)

    copies.append(remote(halo_out.at[0], halo_in.at[0], halo_send.at[0], halo_recv.at[0], (me_d, east)))
    copies.append(remote(halo_out.at[1], halo_in.at[1], halo_send.at[1], halo_recv.at[1], (me_d, west)))
    copies[-2].start()
    copies[-1].start()

    for copy in params_copies:
        copy.wait()

    def woven(rows_144):
        return jnp.concatenate([rows_144[pl.ds(4 + j, 8, stride=16), :] for j in range(24)], axis=0)

    for which in range(3):
        weave[which] = woven(params_t.at[which])

    def spread(table, k):
        return jnp.broadcast_to(table[:, k : k + 1], (WIDE, 128))

    def turn(b):
        return lax.rem(128 - b, 128)

    ages = -(lax.broadcasted_iota(jnp.int32, (1, 128), 1) + 1).astype(F32)

    def full(r):
        return pl.ds(pl.multiple_of(r * WIDE, WIDE), WIDE)

    @pl.loop(0, rows // 8)
    def _(b):
        table = pltpu.roll(weave[0], turn(8 * b), 1)
        for k in range(8):
            r = 8 * b + k
            nat[full(r), :] = jnp.exp(spread(table, k) * ages) * drain_cum[pl.ds(r, 1), :]

    for copy in copies:
        copy.wait()

    carry = jnp.zeros((rows, cells), F32)
    carry_w = jnp.zeros((8, 128), F32)
    carry_e = jnp.zeros((8, 128), F32)
    for k in range(nd - 1, 0, -1):
        used = k <= me_d
        carry = jnp.where(used, summary_in[k, 0] * carry + summary_in[k, 1], carry)
        carry_w = jnp.where(used, strip_in[0, k, 0] * carry_w + strip_in[0, k, 1], carry_w)
        carry_e = jnp.where(used, strip_in[1, k, 0] * carry_e + strip_in[1, k, 1], carry_e)
    carry_t[0:8, :] = carry_w
    carry_t[8:136, :] = turned(carry)
    carry_t[136:144, :] = carry_e
    weave[0] = woven(carry_t)

    def enter_rows(b):
        table = pltpu.roll(weave[0], turn(8 * b), 1)
        for k in range(8):
            r = 8 * b + k
            low, high = halo_in[0, 4 * b + k // 2], halo_in[1, 4 * b + k // 2]
            if k % 2 == 0:
                low = pltpu.roll(low, 4, 0)
            else:
                high = pltpu.roll(high, 4, 0)
            local[r, 0:8, :] = low
            local[r, 136:144, :] = high
            nat[full(r), :] = woven(local.at[r]) + nat[full(r), :] * spread(table, k)
        for which, gains in ((1, gain_self), (2, gain_side)):
            table = pltpu.roll(weave[which], turn(8 * b), 1)
            for k in range(8):
                gains[lax.rem(8 * b + k, kept)] = spread(table, k)

    spot = gathered.at[me_l, :, pl.ds(pl.multiple_of(me_d * days, days), days)]
    mine = pltpu.make_async_copy(blocks.at[me], spot, own_sem)

    def row_copy(k):
        other = lax.rem(me + k, count)
        return remote(
            blocks.at[other], spot, row_send.at[k], row_recv.at[k],
            (other // nl, lax.rem(other, nl)),
        )

    back = me_l < nl // 2

    def row(i):
        return jnp.where(back, rows - 1 - i, i)

    def smooth(p, i, low, high):
        north, south = jnp.maximum(i - 1, low), jnp.minimum(i + 1, high - 1)
        inner = pl.ds(8 * p, WIDE - 16 * p)

        def line(j, start, size):
            if p == 1:
                return nat[pl.ds(pl.multiple_of(row(j) * WIDE + start, 8), size), :]
            return rings[p - 2, lax.rem(j, RING), pl.ds(start, size), :]

        gain = lax.rem(row(i), kept)
        size = WIDE - 16 * p
        here = line(i, 8 * p - 8, size + 16)
        around = (
            here[16:] + here[:-16] + line(north, 8 * p, size) + line(south, 8 * p, size)
        )
        return gain_self[gain, inner, :] * here[8:-8] + gain_side[gain, inner, :] * around

    @pl.loop(0, rows + 4)
    def _(i):
        @pl.when(jnp.logical_and(lax.rem(i, 8) == 0, i < rows))
        def _():
            enter_rows(row(i) // 8)

        for p in range(1, 5):
            j = i - p

            @pl.when(jnp.logical_and(j >= 0, j < rows))
            def _():
                new = smooth(p, j, 0, rows)
                if p < 4:
                    rings[p - 1, lax.rem(j, RING), pl.ds(8 * p, WIDE - 16 * p), :] = new
                else:
                    r = row(j)
                    for v in range(16):
                        plain[pl.ds(v, 8, stride=16), :] = new[8 * v : 8 * v + 8]
                    blocks[r] = plain[...].astype(jnp.bfloat16)

                    @pl.when(r == me)
                    def _():
                        mine.start()

                    @pl.when(r != me)
                    def _():
                        row_copy(lax.rem(r - me + count, count)).start()

    fetch.wait()
    mine.wait()

    def result_copy(tile):
        part = pl.ds(pl.multiple_of(tile * cells, cells), cells)
        return pltpu.make_async_copy(result.at[:, part], out.at[:, part], out_sem.at[tile])

    @pl.loop(0, nl)
    def _(m):
        tile = lax.rem(me_l + m, nl)
        for d in range(nd):
            k = lax.rem(me - d * nl - tile + count, count)

            @pl.when(k > 0)
            def _():
                row_copy(k).wait_recv()

        zone = zones[0, tile]
        result[:, pl.ds(pl.multiple_of(tile * cells, cells), cells)] = lax.dot_general(
            kernels_in[zone], gathered[tile], (((1,), (1,)), ((), ())),
            preferred_element_type=F32,
        ).astype(result.dtype)
        result_copy(tile).start()

    @pl.loop(1, count)
    def _(k):
        row_copy(k).wait_send()

    @pl.loop(0, nl)
    def _(tile):
        result_copy(tile).wait()


def body(nd, nl, observed, decay_rate, drain_factor, smoothing, land_mask, zone_ids, kernels):
    days, rows, cells = observed.shape
    count = nd * nl
    total = kernels.shape[1]
    assert days == 128 and cells == 128 and rows == count
    vmem = pl.BlockSpec(memory_space=pltpu.VMEM)
    dma = pltpu.SemaphoreType.DMA
    kept = min(rows, 16)
    out = pl.pallas_call(
        functools.partial(series_kernel, nd, nl),
        out_shape=jax.ShapeDtypeStruct((total, nl * cells), jnp.bfloat16),
        in_specs=[pl.BlockSpec(memory_space=pltpu.SMEM)] + [vmem] * 5
        + [pl.BlockSpec(memory_space=pl.ANY)],
        out_specs=pl.BlockSpec(memory_space=pl.ANY),
        scratch_shapes=[
            pltpu.VMEM((rows, days), F32),
            pltpu.VMEM((rows * WIDE, cells), F32),
            pltpu.VMEM((rows, 144, days), F32),
            pltpu.VMEM((2, rows, cells), F32),
            pltpu.VMEM((nd, 2, rows, cells), F32),
            pltpu.VMEM((2, cells, 128), F32),
            pltpu.VMEM((2, nd, 2, 8, 128), F32),
            pltpu.VMEM((3, 144, 128), F32),
            pltpu.VMEM((2, rows // 2, 8, days), F32),
            pltpu.VMEM((2, rows // 2, 8, days), F32),
            pltpu.VMEM((3, WIDE, 128), F32),
            pltpu.VMEM((128, 128), F32),
            pltpu.VMEM((kept, WIDE, 128), F32),
            pltpu.VMEM((kept, WIDE, 128), F32),
            pltpu.VMEM((144, 128), F32),
            pltpu.VMEM((3, RING, WIDE, 128), F32),
            pltpu.VMEM((rows, cells, days), jnp.bfloat16),
            pltpu.VMEM(kernels.shape, jnp.bfloat16),
            pltpu.VMEM((nl, cells, total), jnp.bfloat16),
            pltpu.VMEM((total, nl * cells), jnp.bfloat16),
            dma((nd,)), dma((nd,)),
            dma((2, nd)), dma((2, nd)),
            dma((2,)), dma((2,)),
            dma((2,)), dma((2,)),
            dma((count,)), dma((count,)),
            dma, dma, dma((nl,)),
        ],
        compiler_params=pltpu.CompilerParams(
            collective_id=0, has_side_effects=True, vmem_limit_bytes=62 * 2**20
        ),
        name="series",
    )(zone_ids, observed, decay_rate, drain_factor.T, smoothing, land_mask, kernels)
    return out.reshape(total, 1, nl * cells)


def solution(mesh):
    placed = (
        P("day", None, "lon"),
        P(None, "lon"),
        P("day", None),
        P(None, "lon"),
        P(None, "lon"),
        P(("day", "lon"), None),
        P(),
    )
    return jax.shard_map(
        functools.partial(body, mesh.shape["day"], mesh.shape["lon"]),
        mesh=mesh, in_specs=placed, out_specs=P(None, ("day", "lon"), None), check_vma=False,
    )
```
